32 devices in a mesh: parts: 2 (over x), xline: 16 (over z, y, core).
Axes of the slice: x: 2, y: 2, z: 4, core: 2. Of those that a mesh axis runs over, the one named last changes fastest.
Arguments:
- gathers: bfloat16 [4, 96, 96, 256], P('parts', 'xline'), parts along dimension 0, may hold values from -6 to 6
- time_steps: float32 [2], replicated, may hold values from 0.3 to 0.8
- radon_op: bfloat16 [32, 2, 96, 96], P('xline'), may hold values from -0.4375 to 0.4375
Outputs:
- conditioned: bfloat16 [4, 96, 96, 256], P('parts', 'xline'), parts along dimension 0
The draws below stay inside these ranges and needn't reach their ends.
There are 2 independent parts, one for each index of `parts`. The reference program is written for one: setup_inputs(seed, part) draws one part's arguments, and reference() takes and returns one part's arrays. A program takes and returns all parts, laid end to end along the dimension named above; an argument that names none is the same for every part. Nothing has to cross between parts.
All inputs are finite; a program needn't handle non-finite values.
Results may differ from the reference program's by a relative error of at most 0.0072.
Values may be sent and summed in bfloat16 or wider, within the bound.
A program may use at most 128 MiB of HBM per device.

```python
import math
import jax
import jax.numpy as jnp

IL = 2
NO = 96
NZ = 256
STEPS = 2
XL = 96
NF = 32


def steps_of(own_key, shape, split, smallest, largest):
    gain = 1.0
    for position, parts in split:
        draws = jax.random.uniform(jax.random.fold_in(jax.random.fold_in(own_key, 6), position), (parts,), jnp.float32, smallest / len(split), largest / len(split))
        gain = gain * jnp.repeat(jnp.exp(draws), shape[position] // parts).reshape((-1,) + (1,) * (len(shape) - 1 - position))
    return gain


def centred(rng, extent, spread, bound, cuts=(), kind=jnp.bfloat16):
    values = jax.random.normal(rng, extent, jnp.float32) * spread
    if len(cuts) > 0:
        values = steps_of(rng, extent, cuts, -0.22, 0.18) * values
    return jnp.clip(values, min=-bound, max=bound).astype(kind)


def setup_inputs(seed: int = 0, part: int = 0) -> dict:
    streams_of = jax.random.split(jax.random.key(seed), 4)
    own_keys = jax.random.split(jax.random.fold_in(streams_of[3], part), 4)
    gathers = centred(own_keys[0], (IL, XL, NO, NZ), 1.0, 6.0, ((1, 16),))
    time_steps = jnp.clip(jax.random.uniform(streams_of[1], (STEPS,), jnp.float32, 0.3, 0.8), 0.3, 0.8)
    radon_op = centred(streams_of[2], (NF, 2, NO, NO), (2 * NO) ** -0.5, 0.4375, ((0, 16),))
    return dict(gathers=gathers, time_steps=time_steps, radon_op=radon_op)


def diff_depth(field):
    padded = jnp.pad(field, ((0, 0), (0, 0), (0, 0), (1, 1)))
    return 0.5 * (padded[..., 2:] - padded[..., :-2])


def box_depth(field):
    padded = jnp.pad(field, ((0, 0), (0, 0), (0, 0), (1, 1)))
    return (padded[..., :-2] + padded[..., 1:-1] + padded[..., 2:]) / 3.0


def diff_cross(field):
    return 0.5 * (field[:, 2:] - field[:, :-2])


def box_cross(field):
    return (field[:, :-2] + field[:, 1:-1] + field[:, 2:]) / 3.0


def diffuse(extended, tau_value, columns, total):
    inside = ((columns >= 0) & (columns < total)).astype(jnp.float32)[None, :, None, None]
    grad_cross = diff_cross(extended) * inside[:, 1:-1]
    grad_depth = diff_depth(extended[:, 1:-1]) * inside[:, 1:-1]
    tensor_xx = box_cross(box_depth(grad_cross * grad_cross)) * inside[:, 2:-2]
    tensor_xz = box_cross(box_depth(grad_cross * grad_depth)) * inside[:, 2:-2]
    tensor_zz = box_cross(box_depth(grad_depth * grad_depth)) * inside[:, 2:-2]
    norm_term = 1.0 + tensor_xx + tensor_zz
    inner_x = grad_cross[:, 1:-1]
    inner_z = grad_depth[:, 1:-1]
    flux_cross = inner_x - (tensor_xx * inner_x + tensor_xz * inner_z) / norm_term
    flux_depth = inner_z - (tensor_xz * inner_x + tensor_zz * inner_z) / norm_term
    change = diff_cross(flux_cross) + diff_depth(flux_depth[:, 1:-1])
    return (extended[:, 3:-3] + tau_value * change) * inside[:, 3:-3]


def forward_table(depth, bins):
    zeds = jnp.arange(depth, dtype=jnp.int32)[:, None]
    freqs = jnp.arange(bins, dtype=jnp.int32)[None, :]
    phase = ((zeds * freqs) % depth).astype(jnp.float32) * (2.0 * math.pi / depth)
    return jnp.concatenate([jnp.cos(phase), -jnp.sin(phase)], axis=1).astype(jnp.bfloat16)


def inverse_table(depth, bins):
    freqs = jnp.arange(bins, dtype=jnp.int32)[:, None]
    zeds = jnp.arange(depth, dtype=jnp.int32)[None, :]
    phase = ((zeds * freqs) % depth).astype(jnp.float32) * (2.0 * math.pi / depth)
    weight = jnp.where(freqs == 0, 1.0, 2.0).astype(jnp.float32) / depth
    return jnp.concatenate([weight * jnp.cos(phase), -weight * jnp.sin(phase)], axis=0).astype(jnp.bfloat16)


def reference(gathers, time_steps, radon_op):
    field = gathers.astype(jnp.float32)
    width = field.shape[1]
    columns = jnp.arange(-3, width + 3, dtype=jnp.int32)
    for number in range(STEPS):
        extended = jnp.pad(field, ((0, 0), (3, 3), (0, 0), (0, 0)))
        field = diffuse(extended, time_steps[number], columns, width)
    smooth = field.astype(jnp.bfloat16)
    spectrum = jnp.dot(smooth.reshape(-1, NZ), forward_table(NZ, NF), preferred_element_type=jnp.float32)
    spectrum = spectrum.astype(jnp.bfloat16).reshape(-1, NO, 2, NF)
    real_row = jnp.stack([radon_op[:, 0], -radon_op[:, 1]], axis=1)
    imag_row = jnp.stack([radon_op[:, 1], radon_op[:, 0]], axis=1)
    mats = jnp.stack([real_row, imag_row], axis=1)
    filtered = jnp.einsum("aorf,fqrpo->apqf", spectrum.astype(jnp.float32), mats.astype(jnp.float32))
    filtered = filtered.astype(jnp.bfloat16).reshape(-1, 2 * NF)
    result = jnp.dot(filtered, inverse_table(NZ, NF), preferred_element_type=jnp.float32)
    return result.astype(jnp.bfloat16).reshape(IL, XL, NO, NZ)
```

```python
import functools
import math

import jax
import jax.numpy as jnp
import ml_dtypes
import numpy as np
from jax import lax
from jax.experimental import pallas as pl
from jax.experimental.pallas import tpu as pltpu
from jax.sharding import PartitionSpec as P

ROWS = 16


def tables(depth, bins):
    phase = (np.arange(bins)[:, None] * np.arange(depth)[None, :] % depth) * (2.0 * math.pi / depth)
    weight = np.where(np.arange(bins) == 0, 1.0, 2.0)[:, None] / depth
    forward = np.stack([np.cos(phase), -np.sin(phase)], axis=1).reshape(2 * bins, depth)
    inverse = np.stack([weight * np.cos(phase), -weight * np.sin(phase)], axis=1).reshape(2 * bins, depth)
    diff = np.eye(depth, k=-1) - np.eye(depth, k=1)
    box = np.eye(depth, k=-1) + np.eye(depth) + np.eye(depth, k=1)
    return [a.astype(ml_dtypes.bfloat16) for a in (forward, inverse, diff, box)]


def dot(a, b):
    return jnp.dot(a, b, preferred_element_type=jnp.float32)


def dot_on(a, b, left, right):
    return lax.dot_general(a, b, (((left,), (right,)), ((), ())), preferred_element_type=jnp.float32)


def rows_of(line, count=1):
    return pl.ds(line * ROWS, count * ROWS)


def diffuse_step(width, load, keep, tau, last, scratch):
    field_s, half_s, gz_s, prod_s, tens_s, fx_s, fz_s, diff_ref, box_ref = scratch

    def grad(x):
        value = load(x + 1) - load(x - 1)
        return value if keep(x) is None else value * keep(x)

    gz_s[rows_of(0, width - 2), :] = dot(half_s[rows_of(1, width - 2), :], diff_ref[...])
    older = []
    for x in range(1, width - 1):
        gx, gz = grad(x), gz_s[rows_of(x - 1), :]
        older.append((gx * gx, gx * gz, gz * gz))
        if len(older) == 3:
            for number in range(3):
                total = older[0][number] + older[1][number] + older[2][number]
                prod_s[number, rows_of(x - 3), :] = total.astype(jnp.bfloat16)
            older.pop(0)
    for number in range(3):
        tens_s[number, rows_of(0, width - 4), :] = dot(
            prod_s[number, rows_of(0, width - 4), :], box_ref[...]
        )
    for x in range(2, width - 2):
        gx, gz = grad(x), gz_s[rows_of(x - 1), :]
        sxx, sxz, szz = (tens_s[number, rows_of(x - 2), :] for number in range(3))
        inverse = pl.reciprocal(36.0 + sxx + szz, approx=True)
        fx_s[rows_of(x - 2), :] = gx - (sxx * gx + sxz * gz) * inverse
        if 3 <= x < width - 3:
            fz_s[rows_of(x - 3), :] = (gz - (sxz * gx + szz * gz) * inverse).astype(jnp.bfloat16)
    gz_s[rows_of(0, width - 6), :] = dot(fz_s[rows_of(0, width - 6), :], diff_ref[...])
    for x in range(3, width - 3):
        change = fx_s[rows_of(x - 1), :] - fx_s[rows_of(x - 3), :] + gz_s[rows_of(x - 3), :]
        value = load(x) + tau * change
        if keep(x) is not None:
            value = value * keep(x)
        if last:
            yield x - 3, value
        else:
            field_s[rows_of(x - 3), :] = value
            half_s[rows_of(x - 3), :] = value.astype(jnp.bfloat16)


def kernel(
    tau_ref, own_ref, left_ref, right_ref, radon_ref, forward_ref, inverse_ref, diff_ref, box_ref,
    out_ref, first_s, field_s, half_s, gz_s, prod_s, tens_s, fx_s, fz_s, smooth_s, spec_s, filt_s,
):
    inlines, lines, offsets, depth = own_ref.shape
    halo = left_ref.shape[1]
    steps = halo // 3
    bins = radon_ref.shape[0]
    me = lax.axis_index("xline")
    keep_left = jnp.where(me > 0, 1.0, 0.0).astype(jnp.float32)
    keep_right = jnp.where(me < lax.axis_size("xline") - 1, 1.0, 0.0).astype(jnp.float32)
    scratch = (field_s, half_s, gz_s, prod_s, tens_s, fx_s, fz_s, diff_ref, box_ref)
    blocks = offsets // ROWS

    def chunk(number, carry):
        inline = number // blocks
        at = pl.ds(pl.multiple_of(number % blocks * ROWS, ROWS), ROWS)
        for x in range(halo):
            half_s[rows_of(x), :] = left_ref[inline, x, at, :]
            half_s[rows_of(halo + lines + x), :] = right_ref[inline, x, at, :]
        for x in range(lines):
            half_s[rows_of(halo + x), :] = own_ref[inline, x, at, :]
        first_s[...] = half_s[...].astype(jnp.float32)
        for step in range(steps):
            width = lines + 2 * (halo - 3 * step)
            border = halo - 3 * step

            def keep(x):
                if x < border:
                    return keep_left
                return keep_right if x >= border + lines else None

            source = first_s if step == 0 else field_s
            results = diffuse_step(
                width, lambda x: source[rows_of(x), :], keep, 0.25 * tau_ref[step],
                step == steps - 1, scratch,
            )
            for x, value in results:
                smooth_s[inline * lines + x, at, :] = value.astype(jnp.bfloat16)
        return carry

    lax.fori_loop(0, inlines * blocks, chunk, 0)

    count = inlines * lines
    slots = spec_s.shape[0] // (2 * bins)
    for n in range(count):
        value = dot_on(forward_ref[...], smooth_s[n], 1, 1)
        spec_s[pl.ds(n, 2 * bins, stride=slots), :] = value.astype(jnp.bfloat16).astype(jnp.float32)

    def one_bin(k, carry):
        base = pl.multiple_of(k * 2 * slots, 2 * slots)
        both = spec_s[pl.ds(base, 2 * slots), :].astype(jnp.bfloat16)
        by_real = dot_on(both, radon_ref[k, 0], 1, 1)
        by_imag = dot_on(both, radon_ref[k, 1], 1, 1)
        real = by_real[:slots] - by_imag[slots:]
        imag = by_imag[:slots] + by_real[slots:]
        filt_s[pl.ds(base, slots), :] = real.astype(jnp.bfloat16).astype(jnp.float32)
        filt_s[pl.ds(base + slots, slots), :] = imag.astype(jnp.bfloat16).astype(jnp.float32)
        return carry

    lax.fori_loop(0, bins, one_bin, 0, unroll=8)
    for n in range(count):
        value = filt_s[pl.ds(n, 2 * bins, stride=slots), :].astype(jnp.bfloat16)
        result = dot_on(value, inverse_ref[...], 0, 0)
        out_ref[n // lines, n % lines] = result.astype(jnp.bfloat16)


def per_device(gathers, time_steps, radon_op):
    inlines, lines, offsets, depth = gathers.shape
    devices = lax.axis_size("xline")
    bins = radon_op.shape[0] * devices
    halo = 3 * time_steps.shape[0]
    operators = lax.all_gather(radon_op, "xline", axis=0, tiled=True)
    left = lax.ppermute(
        gathers[:, lines - halo :], "xline", [(d, d + 1) for d in range(devices - 1)]
    )
    right = lax.ppermute(gathers[:, :halo], "xline", [(d + 1, d) for d in range(devices - 1)])
    width = lines + 2 * halo
    slots = -(-inlines * lines // 16) * 16
    vmem = pl.BlockSpec(memory_space=pltpu.VMEM)
    f32, bf16 = jnp.float32, jnp.bfloat16
    return pl.pallas_call(
        kernel,
        out_shape=jax.ShapeDtypeStruct(gathers.shape, bf16),
        in_specs=[pl.BlockSpec(memory_space=pltpu.SMEM)] + [vmem] * 8,
        out_specs=vmem,
        scratch_shapes=[
            pltpu.VMEM((width * ROWS, depth), f32),
            pltpu.VMEM((width * ROWS, depth), f32),
            pltpu.VMEM((width * ROWS, depth), bf16),
            pltpu.VMEM((width * ROWS, depth), f32),
            pltpu.VMEM((3, width * ROWS, depth), bf16),
            pltpu.VMEM((3, width * ROWS, depth), f32),
            pltpu.VMEM((width * ROWS, depth), f32),
            pltpu.VMEM((width * ROWS, depth), bf16),
            pltpu.VMEM((inlines * lines, offsets, depth), bf16),
            pltpu.VMEM((2 * bins * slots, offsets), f32),
            pltpu.VMEM((2 * bins * slots, offsets), f32),
        ],
        compiler_params=pltpu.CompilerParams(vmem_limit_bytes=48 * 2**20),
    )(time_steps, gathers, left, right, operators, *tables(depth, bins))


def solution(mesh):
    return jax.shard_map(
        per_device,
        mesh=mesh,
        in_specs=(P("parts", "xline", None, None), P(), P("xline", None, None, None)),
        out_specs=P("parts", "xline", None, None),
        check_vma=False,
    )
```

```python
import functools
import math

import jax
import jax.numpy as jnp
import ml_dtypes
import numpy as np
from jax import lax
from jax.experimental import pallas as pl
from jax.experimental.pallas import tpu as pltpu
from jax.sharding import PartitionSpec as P

MESH = pl.DeviceIdType.MESH
ROWS = 16


def tables(depth, bins):
    phase = (np.arange(bins)[:, None] * np.arange(depth)[None, :] % depth) * (2.0 * math.pi / depth)
    weight = np.where(np.arange(bins) == 0, 1.0, 2.0)[:, None] / depth
    forward = np.stack([np.cos(phase), -np.sin(phase)], axis=1).reshape(2 * bins, depth)
    inverse = np.stack([weight * np.cos(phase), -weight * np.sin(phase)], axis=1).reshape(2 * bins, depth)
    diff = np.eye(depth, k=-1) - np.eye(depth, k=1)
    box = np.eye(depth, k=-1) + np.eye(depth) + np.eye(depth, k=1)
    return [a.astype(ml_dtypes.bfloat16) for a in (forward, inverse, diff, box)]


def dot(a, b):
    return jnp.dot(a, b, preferred_element_type=jnp.float32)


def dot_on(a, b, left, right):
    return lax.dot_general(a, b, (((left,), (right,)), ((), ())), preferred_element_type=jnp.float32)


def rows_of(line, count=1):
    return pl.ds(line * ROWS, count * ROWS)


def diffuse_step(width, load, keep, tau, last, scratch):
    field_s, half_s, gz_s, prod_s, tens_s, fx_s, fz_s, diff_ref, box_ref = scratch

    def grad(x):
        value = load(x + 1) - load(x - 1)
        return value if keep(x) is None else value * keep(x)

    gz_s[rows_of(0, width - 2), :] = dot(half_s[rows_of(1, width - 2), :], diff_ref[...])
    older = []
    for x in range(1, width - 1):
        gx, gz = grad(x), gz_s[rows_of(x - 1), :]
        older.append((gx * gx, gx * gz, gz * gz))
        if len(older) == 3:
            for number in range(3):
                total = older[0][number] + older[1][number] + older[2][number]
                prod_s[number, rows_of(x - 3), :] = total.astype(jnp.bfloat16)
            older.pop(0)
    for number in range(3):
        tens_s[number, rows_of(0, width - 4), :] = dot(
            prod_s[number, rows_of(0, width - 4), :], box_ref[...]
        )
    for x in range(2, width - 2):
        gx, gz = grad(x), gz_s[rows_of(x - 1), :]
        sxx, sxz, szz = (tens_s[number, rows_of(x - 2), :] for number in range(3))
        inverse = pl.reciprocal(36.0 + sxx + szz, approx=True)
        fx_s[rows_of(x - 2), :] = gx - (sxx * gx + sxz * gz) * inverse
        if 3 <= x < width - 3:
            fz_s[rows_of(x - 3), :] = (gz - (sxz * gx + szz * gz) * inverse).astype(jnp.bfloat16)
    gz_s[rows_of(0, width - 6), :] = dot(fz_s[rows_of(0, width - 6), :], diff_ref[...])
    for x in range(3, width - 3):
        change = fx_s[rows_of(x - 1), :] - fx_s[rows_of(x - 3), :] + gz_s[rows_of(x - 3), :]
        value = load(x) + tau * change
        if keep(x) is not None:
            value = value * keep(x)
        if last:
            yield x - 3, value
        else:
            field_s[rows_of(x - 3), :] = value
            half_s[rows_of(x - 3), :] = value.astype(jnp.bfloat16)


def kernel(
    tau_ref, own_hbm, radon_hbm, table_hbm, out_ref,
    own_ref, left_ref, right_ref, radon_ref, table_ref,
    first_s, field_s, half_s, gz_s, prod_s, tens_s, fx_s, fz_s, smooth_s, spec_s, filt_s,
    local_sem, halo_send, halo_recv, radon_send, radon_recv,
):
    inlines, lines, offsets, depth = own_ref.shape
    halo = left_ref.shape[1]
    steps = halo // 3
    bins = radon_ref.shape[0]
    share = radon_hbm.shape[0]
    devices = bins // share
    chips = devices // 2
    me = lax.axis_index("xline")
    chip, core = me // 2, me % 2
    sibling = chip * 2 + 1 - core

    barrier = pltpu.get_barrier_semaphore()

    def greet(j, carry):
        pl.semaphore_signal(
            barrier, inc=1, device_id={"xline": (me + j) % devices}, device_id_type=MESH
        )
        return carry

    lax.fori_loop(1, devices, greet, 0)

    block = pl.ds(pl.multiple_of(me * share, share), share)
    local = [
        pltpu.make_async_copy(own_hbm, own_ref, local_sem.at[0]),
        pltpu.make_async_copy(table_hbm, table_ref, local_sem.at[1]),
        pltpu.make_async_copy(radon_hbm, radon_ref.at[block], local_sem.at[2]),
    ]
    for copy in local:
        copy.start()

    @pl.when(me == 0)
    def _():
        left_ref[...] = jnp.zeros_like(left_ref)

    @pl.when(me == devices - 1)
    def _():
        right_ref[...] = jnp.zeros_like(right_ref)

    pl.semaphore_wait(barrier, devices - 1)

    def to_right(inline):
        return pltpu.make_async_remote_copy(
            src_ref=own_hbm.at[inline, pl.ds(lines - halo, halo)],
            dst_ref=left_ref.at[inline],
            send_sem=halo_send.at[0, inline],
            recv_sem=halo_recv.at[0, inline],
            device_id={"xline": (me + 1) % devices},
            device_id_type=MESH,
        )

    def to_left(inline):
        return pltpu.make_async_remote_copy(
            src_ref=own_hbm.at[inline, pl.ds(0, halo)],
            dst_ref=right_ref.at[inline],
            send_sem=halo_send.at[1, inline],
            recv_sem=halo_recv.at[1, inline],
            device_id={"xline": (me + devices - 1) % devices},
            device_id_type=MESH,
        )

    def send_halo(inline):
        @pl.when(me < devices - 1)
        def _():
            to_right(inline).start()

        @pl.when(me > 0)
        def _():
            to_left(inline).start()

    def spread(target):
        return pltpu.make_async_remote_copy(
            src_ref=radon_hbm,
            dst_ref=radon_ref.at[block],
            send_sem=radon_send.at[target],
            recv_sem=radon_recv.at[me],
            device_id={"xline": target},
            device_id_type=MESH,
        )

    def forward(source):
        held = radon_ref.at[pl.ds(pl.multiple_of(source * share, share), share)]
        return pltpu.make_async_remote_copy(
            src_ref=held,
            dst_ref=held,
            send_sem=radon_send.at[source + 1 - 2 * core],
            recv_sem=radon_recv.at[source],
            device_id={"xline": sibling},
            device_id_type=MESH,
        )

    def same_core(j):
        return (chip + j) % chips * 2 + core

    def each_chip(action):
        def body(j, carry):
            action(same_core(j))
            return carry

        lax.fori_loop(1, chips, body, 0)

    send_halo(0)
    each_chip(lambda target: spread(target).start())
    spread(sibling).start()
    for inline in range(1, inlines):
        send_halo(inline)
    for copy in local:
        copy.wait()

    diff_ref = table_ref.at[pl.ds(4 * bins, depth)]
    box_ref = table_ref.at[pl.ds(4 * bins + depth, depth)]
    keep_left = jnp.where(me > 0, 1.0, 0.0).astype(jnp.float32)
    keep_right = jnp.where(me < devices - 1, 1.0, 0.0).astype(jnp.float32)
    scratch = (field_s, half_s, gz_s, prod_s, tens_s, fx_s, fz_s, diff_ref, box_ref)
    blocks = offsets // ROWS

    def chunk(inline, number):
        at = pl.ds(pl.multiple_of(number * ROWS, ROWS), ROWS)
        for x in range(halo):
            half_s[rows_of(x), :] = left_ref[inline, x, at, :]
            half_s[rows_of(halo + lines + x), :] = right_ref[inline, x, at, :]
        for x in range(lines):
            half_s[rows_of(halo + x), :] = own_ref[inline, x, at, :]
        first_s[...] = half_s[...].astype(jnp.float32)
        for step in range(steps):
            width = lines + 2 * (halo - 3 * step)
            border = halo - 3 * step

            def keep(x):
                if x < border:
                    return keep_left
                return keep_right if x >= border + lines else None

            source = first_s if step == 0 else field_s
            results = diffuse_step(
                width, lambda x: source[rows_of(x), :], keep, 0.25 * tau_ref[step],
                step == steps - 1, scratch,
            )
            for x, value in results:
                smooth_s[inline * lines + x, at, :] = value.astype(jnp.bfloat16)
        return inline

    for inline in range(inlines):

        @pl.when(me > 0)
        def _():
            to_right(inline).wait_recv()

        @pl.when(me < devices - 1)
        def _():
            to_left(inline).wait_recv()

        def one(number, carry):
            chunk(inline, number)
            return carry

        lax.fori_loop(0, blocks, one, 0)
        if inline == 0:

            def pass_on(source):
                forward(source).wait_recv()
                forward(source).start()

            each_chip(pass_on)

    count = inlines * lines
    slots = spec_s.shape[0] // (2 * bins)
    for n in range(count):
        value = dot_on(table_ref[pl.ds(0, 2 * bins), :], smooth_s[n], 1, 1)
        spec_s[pl.ds(n, 2 * bins, stride=slots), :] = value.astype(jnp.bfloat16).astype(jnp.float32)

    forward(sibling).wait_recv()
    each_chip(lambda source: forward(source + 1 - 2 * core).wait_recv())

    def one_bin(k, carry):
        base = pl.multiple_of(k * 2 * slots, 2 * slots)
        both = spec_s[pl.ds(base, 2 * slots), :].astype(jnp.bfloat16)
        by_real = dot_on(both, radon_ref[k, 0], 1, 1)
        by_imag = dot_on(both, radon_ref[k, 1], 1, 1)
        real = by_real[:slots] - by_imag[slots:]
        imag = by_imag[:slots] + by_real[slots:]
        filt_s[pl.ds(base, slots), :] = real.astype(jnp.bfloat16).astype(jnp.float32)
        filt_s[pl.ds(base + slots, slots), :] = imag.astype(jnp.bfloat16).astype(jnp.float32)
        return carry

    lax.fori_loop(0, bins, one_bin, 0, unroll=8)
    for n in range(count):
        value = filt_s[pl.ds(n, 2 * bins, stride=slots), :].astype(jnp.bfloat16)
        result = dot_on(value, table_ref[pl.ds(2 * bins, 2 * bins), :], 0, 0)
        out_ref[n // lines, n % lines] = result.astype(jnp.bfloat16)

    for inline in range(inlines):

        @pl.when(me < devices - 1)
        def _():
            to_right(inline).wait_send()

        @pl.when(me > 0)
        def _():
            to_left(inline).wait_send()

    spread(sibling).wait_send()

    def finish(peer):
        spread(peer).wait_send()
        forward(peer).wait_send()

    each_chip(finish)


def per_device(gathers, time_steps, radon_op):
    inlines, lines, offsets, depth = gathers.shape
    devices = lax.axis_size("xline")
    bins = radon_op.shape[0] * devices
    halo = 3 * time_steps.shape[0]
    width = lines + 2 * halo
    slots = -(-inlines * lines // 16) * 16
    table = np.concatenate(tables(depth, bins), axis=0)
    hbm = pl.BlockSpec(memory_space=pl.ANY)
    f32, bf16 = jnp.float32, jnp.bfloat16
    return pl.pallas_call(
        kernel,
        out_shape=jax.ShapeDtypeStruct(gathers.shape, bf16),
        in_specs=[pl.BlockSpec(memory_space=pltpu.SMEM), hbm, hbm, hbm],
        out_specs=pl.BlockSpec(memory_space=pltpu.VMEM),
        scratch_shapes=[
            pltpu.VMEM(gathers.shape, bf16),
            pltpu.VMEM((inlines, halo, offsets, depth), bf16),
            pltpu.VMEM((inlines, halo, offsets, depth), bf16),
            pltpu.VMEM((bins,) + radon_op.shape[1:], bf16),
            pltpu.VMEM(table.shape, bf16),
            pltpu.VMEM((width * ROWS, depth), f32),
            pltpu.VMEM((width * ROWS, depth), f32),
            pltpu.VMEM((width * ROWS, depth), bf16),
            pltpu.VMEM((width * ROWS, depth), f32),
            pltpu.VMEM((3, width * ROWS, depth), bf16),
            pltpu.VMEM((3, width * ROWS, depth), f32),
            pltpu.VMEM((width * ROWS, depth), f32),
            pltpu.VMEM((width * ROWS, depth), bf16),
            pltpu.VMEM((inlines * lines, offsets, depth), bf16),
            pltpu.VMEM((2 * bins * slots, offsets), f32),
            pltpu.VMEM((2 * bins * slots, offsets), f32),
            pltpu.SemaphoreType.DMA((3,)),
            pltpu.SemaphoreType.DMA((2, inlines)),
            pltpu.SemaphoreType.DMA((2, inlines)),
            pltpu.SemaphoreType.DMA((devices,)),
            pltpu.SemaphoreType.DMA((devices,)),
        ],
        compiler_params=pltpu.CompilerParams(
            collective_id=0, has_side_effects=True, vmem_limit_bytes=48 * 2**20
        ),
    )(time_steps, gathers, radon_op, table)


def solution(mesh):
    return jax.shard_map(
        per_device,
        mesh=mesh,
        in_specs=(P("parts", "xline", None, None), P(), P("xline", None, None, None)),
        out_specs=P("parts", "xline", None, None),
        check_vma=False,
    )
```

```python
import functools
import math

import jax
import jax.numpy as jnp
import ml_dtypes
import numpy as np
from jax import lax
from jax.experimental import pallas as pl
from jax.experimental.pallas import tpu as pltpu
from jax.sharding import PartitionSpec as P

MESH = pl.DeviceIdType.MESH
ROWS = 48


def tables(depth, bins):
    phase = (np.arange(bins)[:, None] * np.arange(depth)[None, :] % depth) * (2.0 * math.pi / depth)
    weight = np.where(np.arange(bins) == 0, 1.0, 2.0)[:, None] / depth
    forward = np.stack([np.cos(phase), -np.sin(phase)], axis=1).reshape(2 * bins, depth)
    inverse = np.stack([weight * np.cos(phase), -weight * np.sin(phase)], axis=1).reshape(2 * bins, depth)
    diff = np.eye(depth, k=-1) - np.eye(depth, k=1)
    box = np.eye(depth, k=-1) + np.eye(depth) + np.eye(depth, k=1)
    return [a.astype(ml_dtypes.bfloat16) for a in (forward, inverse, diff, box)]


def dot(a, b):
    return jnp.dot(a, b, preferred_element_type=jnp.float32)


def dot_on(a, b, left, right):
    return lax.dot_general(a, b, (((left,), (right,)), ((), ())), preferred_element_type=jnp.float32)


def rows_of(line, count=1):
    return pl.ds(line * ROWS, count * ROWS)


def diffuse_step(width, load, keep, tau, last, scratch):
    field_s, half_s, gz_s, prod_s, tens_s, fx_s, fz_s, diff_ref, box_ref = scratch

    def grad(x):
        value = load(x + 1) - load(x - 1)
        return value if keep(x) is None else value * keep(x)

    gz_s[rows_of(0, width - 2), :] = dot(half_s[rows_of(1, width - 2), :], diff_ref[...])
    older = []
    for x in range(1, width - 1):
        gx, gz = grad(x), gz_s[rows_of(x - 1), :]
        older.append((gx * gx, gx * gz, gz * gz))
        if len(older) == 3:
            for number in range(3):
                total = older[0][number] + older[1][number] + older[2][number]
                prod_s[number, rows_of(x - 3), :] = total.astype(jnp.bfloat16)
            older.pop(0)
    for number in range(3):
        tens_s[number, rows_of(0, width - 4), :] = dot(
            prod_s[number, rows_of(0, width - 4), :], box_ref[...]
        )
    for x in range(2, width - 2):
        gx, gz = grad(x), gz_s[rows_of(x - 1), :]
        sxx, sxz, szz = (tens_s[number, rows_of(x - 2), :] for number in range(3))
        inverse = pl.reciprocal(36.0 + sxx + szz, approx=True)
        fx_s[rows_of(x - 2), :] = gx - (sxx * gx + sxz * gz) * inverse
        if 3 <= x < width - 3:
            fz_s[rows_of(x - 3), :] = (gz - (sxz * gx + szz * gz) * inverse).astype(jnp.bfloat16)
    gz_s[rows_of(0, width - 6), :] = dot(fz_s[rows_of(0, width - 6), :], diff_ref[...])
    for x in range(3, width - 3):
        change = fx_s[rows_of(x - 1), :] - fx_s[rows_of(x - 3), :] + gz_s[rows_of(x - 3), :]
        value = load(x) + tau * change
        if keep(x) is not None:
            value = value * keep(x)
        if last:
            yield x - 3, value
        else:
            field_s[rows_of(x - 3), :] = value
            half_s[rows_of(x - 3), :] = value.astype(jnp.bfloat16)


def kernel(
    tau_ref, own_hbm, radon_hbm, table_hbm, out_ref,
    own_ref, left_ref, right_ref, radon_ref, table_ref,
    first_s, field_s, half_s, gz_s, prod_s, tens_s, fx_s, fz_s, smooth_s, spec_s, filt_s,
    local_sem, halo_send, halo_recv, radon_send, radon_recv,
):
    inlines, lines, offsets, depth = own_ref.shape
    halo = left_ref.shape[1]
    steps = halo // 3
    bins = radon_ref.shape[0]
    share = radon_hbm.shape[0]
    devices = bins // share
    chips = devices // 2
    me = lax.axis_index("xline")
    chip, core = me // 2, me % 2
    sibling = chip * 2 + 1 - core

    barrier = pltpu.get_barrier_semaphore()

    def greet(j, carry):
        pl.semaphore_signal(
            barrier, inc=1, device_id={"xline": (me + j) % devices}, device_id_type=MESH
        )
        return carry

    lax.fori_loop(1, devices, greet, 0)

    block = pl.ds(pl.multiple_of(me * share, share), share)
    local = [
        pltpu.make_async_copy(own_hbm, own_ref, local_sem.at[0]),
        pltpu.make_async_copy(table_hbm, table_ref, local_sem.at[1]),
        pltpu.make_async_copy(radon_hbm, radon_ref.at[block], local_sem.at[2]),
    ]
    for copy in local:
        copy.start()

    @pl.when(me == 0)
    def _():
        left_ref[...] = jnp.zeros_like(left_ref)

    @pl.when(me == devices - 1)
    def _():
        right_ref[...] = jnp.zeros_like(right_ref)

    pl.semaphore_wait(barrier, devices - 1)

    def to_right(inline):
        return pltpu.make_async_remote_copy(
            src_ref=own_hbm.at[inline, pl.ds(lines - halo, halo)],
            dst_ref=left_ref.at[inline],
            send_sem=halo_send.at[0, inline],
            recv_sem=halo_recv.at[0, inline],
            device_id={"xline": (me + 1) % devices},
            device_id_type=MESH,
        )

    def to_left(inline):
        return pltpu.make_async_remote_copy(
            src_ref=own_hbm.at[inline, pl.ds(0, halo)],
            dst_ref=right_ref.at[inline],
            send_sem=halo_send.at[1, inline],
            recv_sem=halo_recv.at[1, inline],
            device_id={"xline": (me + devices - 1) % devices},
            device_id_type=MESH,
        )

    def send_halo(inline):
        @pl.when(me < devices - 1)
        def _():
            to_right(inline).start()

        @pl.when(me > 0)
        def _():
            to_left(inline).start()

    def spread(target):
        return pltpu.make_async_remote_copy(
            src_ref=radon_hbm,
            dst_ref=radon_ref.at[block],
            send_sem=radon_send.at[target],
            recv_sem=radon_recv.at[me],
            device_id={"xline": target},
            device_id_type=MESH,
        )

    def forward(source):
        held = radon_ref.at[pl.ds(pl.multiple_of(source * share, share), share)]
        return pltpu.make_async_remote_copy(
            src_ref=held,
            dst_ref=held,
            send_sem=radon_send.at[source + 1 - 2 * core],
            recv_sem=radon_recv.at[source],
            device_id={"xline": sibling},
            device_id_type=MESH,
        )

    def same_core(j):
        return (chip + j) % chips * 2 + core

    def each_chip(action):
        def body(j, carry):
            action(same_core(j))
            return carry

        lax.fori_loop(1, chips, body, 0)

    send_halo(0)
    for inline in range(1, inlines):
        send_halo(inline)
    each_chip(lambda target: spread(target).start())
    spread(sibling).start()
    for copy in local:
        copy.wait()

    diff_ref = table_ref.at[pl.ds(4 * bins, depth)]
    box_ref = table_ref.at[pl.ds(4 * bins + depth, depth)]
    keep_left = jnp.where(me > 0, 1.0, 0.0).astype(jnp.float32)
    keep_right = jnp.where(me < devices - 1, 1.0, 0.0).astype(jnp.float32)
    scratch = (field_s, half_s, gz_s, prod_s, tens_s, fx_s, fz_s, diff_ref, box_ref)
    blocks = offsets // ROWS

    def chunk(inline, number):
        at = pl.ds(pl.multiple_of(number * ROWS, ROWS), ROWS)
        for x in range(halo):
            half_s[rows_of(x), :] = left_ref[inline, x, at, :]
            half_s[rows_of(halo + lines + x), :] = right_ref[inline, x, at, :]
        for x in range(lines):
            half_s[rows_of(halo + x), :] = own_ref[inline, x, at, :]
        first_s[...] = half_s[...].astype(jnp.float32)
        for step in range(steps):
            width = lines + 2 * (halo - 3 * step)
            border = halo - 3 * step

            def keep(x):
                if x < border:
                    return keep_left
                return keep_right if x >= border + lines else None

            source = first_s if step == 0 else field_s
            results = diffuse_step(
                width, lambda x: source[rows_of(x), :], keep, 0.25 * tau_ref[step],
                step == steps - 1, scratch,
            )
            for x, value in results:
                smooth_s[inline * lines + x, at, :] = value.astype(jnp.bfloat16)
        return inline

    for inline in range(inlines):

        @pl.when(me > 0)
        def _():
            to_right(inline).wait_recv()

        @pl.when(me < devices - 1)
        def _():
            to_left(inline).wait_recv()

        def one(number, carry):
            chunk(inline, number)
            return carry

        lax.fori_loop(0, blocks, one, 0)
        if inline == inlines - 1:

            def pass_on(source):
                forward(source).wait_recv()
                forward(source).start()

            each_chip(pass_on)

    count = inlines * lines
    slots = spec_s.shape[0] // (2 * bins)
    for n in range(count):
        value = dot_on(table_ref[pl.ds(0, 2 * bins), :], smooth_s[n], 1, 1)
        spec_s[pl.ds(n, 2 * bins, stride=slots), :] = value.astype(jnp.bfloat16).astype(jnp.float32)

    forward(sibling).wait_recv()
    each_chip(lambda source: forward(source + 1 - 2 * core).wait_recv())

    def one_bin(k, carry):
        base = pl.multiple_of(k * 2 * slots, 2 * slots)
        both = spec_s[pl.ds(base, 2 * slots), :].astype(jnp.bfloat16)
        by_real = dot_on(both, radon_ref[k, 0], 1, 1)
        by_imag = dot_on(both, radon_ref[k, 1], 1, 1)
        real = by_real[:slots] - by_imag[slots:]
        imag = by_imag[:slots] + by_real[slots:]
        filt_s[pl.ds(base, slots), :] = real.astype(jnp.bfloat16).astype(jnp.float32)
        filt_s[pl.ds(base + slots, slots), :] = imag.astype(jnp.bfloat16).astype(jnp.float32)
        return carry

    lax.fori_loop(0, bins, one_bin, 0, unroll=8)
    for n in range(count):
        value = filt_s[pl.ds(n, 2 * bins, stride=slots), :].astype(jnp.bfloat16)
        result = dot_on(value, table_ref[pl.ds(2 * bins, 2 * bins), :], 0, 0)
        out_ref[n // lines, n % lines] = result.astype(jnp.bfloat16)

    for inline in range(inlines):

        @pl.when(me < devices - 1)
        def _():
            to_right(inline).wait_send()

        @pl.when(me > 0)
        def _():
            to_left(inline).wait_send()

    spread(sibling).wait_send()

    def finish(peer):
        spread(peer).wait_send()
        forward(peer).wait_send()

    each_chip(finish)


def per_device(gathers, time_steps, radon_op):
    inlines, lines, offsets, depth = gathers.shape
    devices = lax.axis_size("xline")
    bins = radon_op.shape[0] * devices
    halo = 3 * time_steps.shape[0]
    width = lines + 2 * halo
    slots = -(-inlines * lines // 16) * 16
    table = np.concatenate(tables(depth, bins), axis=0)
    hbm = pl.BlockSpec(memory_space=pl.ANY)
    f32, bf16 = jnp.float32, jnp.bfloat16
    return pl.pallas_call(
        kernel,
        out_shape=jax.ShapeDtypeStruct(gathers.shape, bf16),
        in_specs=[pl.BlockSpec(memory_space=pltpu.SMEM), hbm, hbm, hbm],
        out_specs=pl.BlockSpec(memory_space=pltpu.VMEM),
        scratch_shapes=[
            pltpu.VMEM(gathers.shape, bf16),
            pltpu.VMEM((inlines, halo, offsets, depth), bf16),
            pltpu.VMEM((inlines, halo, offsets, depth), bf16),
            pltpu.VMEM((bins,) + radon_op.shape[1:], bf16),
            pltpu.VMEM(table.shape, bf16),
            pltpu.VMEM((width * ROWS, depth), f32),
            pltpu.VMEM((width * ROWS, depth), f32),
            pltpu.VMEM((width * ROWS, depth), bf16),
            pltpu.VMEM((width * ROWS, depth), f32),
            pltpu.VMEM((3, width * ROWS, depth), bf16),
            pltpu.VMEM((3, width * ROWS, depth), f32),
            pltpu.VMEM((width * ROWS, depth), f32),
            pltpu.VMEM((width * ROWS, depth), bf16),
            pltpu.VMEM((inlines * lines, offsets, depth), bf16),
            pltpu.VMEM((2 * bins * slots, offsets), f32),
            pltpu.VMEM((2 * bins * slots, offsets), f32),
            pltpu.SemaphoreType.DMA((3,)),
            pltpu.SemaphoreType.DMA((2, inlines)),
            pltpu.SemaphoreType.DMA((2, inlines)),
            pltpu.SemaphoreType.DMA((devices,)),
            pltpu.SemaphoreType.DMA((devices,)),
        ],
        compiler_params=pltpu.CompilerParams(
            collective_id=0, has_side_effects=True, vmem_limit_bytes=63 * 2**20
        ),
    )(time_steps, gathers, radon_op, table)


def solution(mesh):
    return jax.shard_map(
        per_device,
        mesh=mesh,
        in_specs=(P("parts", "xline", None, None), P(), P("xline", None, None, None)),
        out_specs=P("parts", "xline", None, None),
        check_vma=False,
    )
```
